256 devices in a mesh: ex: 16 (over z_hi, y, core), feat: 16 (over x, z_lo).
Axes of the slice: x: 4, y: 4, z: 8 (z_hi: 2, z_lo: 4; z = z_hi * 4 + z_lo), core: 2. Of those that a mesh axis runs over, the one named last changes fastest.
Arguments:
- activations: bfloat16 [6144, 28672], P('ex', 'feat'), may hold values from -13 to 13
- out_grads: bfloat16 [6144, 8192], P('ex', 'feat'), may hold values from -13 to 13
- lengths: int32 [16], P('ex'), may hold values from 96 to 384, as said below
Outputs:
- kernel: float32 [16, 16], P('ex')
The draws below stay inside these ranges and needn't reach their ends.
Inputs may be any that keep to these rules, and one draw needn't show every extreme that they name: `lengths`: each sequence has at least 96 valid tokens, and some sequence is full.
All inputs are finite; a program needn't handle non-finite values.
Results may differ from the reference program's by a relative error of at most 0.0003.
Values may be sent and summed in bfloat16 or wider, within the bound.
A program may use at most 64 MiB of HBM per device.

```python
import math
import jax
import jax.numpy as jnp
from jax import lax

FF = 28672
D = 8192
LEN = 384
SEQS = 16
TOKENS = 6144


def shared_latent(key, scale_low, scale_high):
    key = jax.random.fold_in(key, 5)
    key_coef, key_scale = jax.random.split(key)
    latent_count = min(512, D // 2)
    coefs = jnp.clip(jax.random.normal(key_coef, (TOKENS, latent_count), jnp.float32), -3.0, 3.0)
    seq_scale = jnp.exp(jax.random.uniform(key_scale, (SEQS, latent_count), jnp.float32, math.log(scale_low), math.log(scale_high)))
    return coefs * jnp.repeat(seq_scale, LEN, axis=0)


def mixed_rows(key, latent, width, noise_part):
    key_map, key_gain = jax.random.split(key)
    latent_count = latent.shape[1]
    group = (jax.random.permutation(key_map, width) % latent_count).astype(jnp.int32)
    gains = jax.random.uniform(key_gain, (width,), jnp.float32, 0.6, 1.4)
    signal = 0.9 * jnp.take(latent, group, axis=1) * gains[None, :]
    return jnp.clip(signal + noise_part, -12.5, 12.5)


def draw_activations(key, part):
    latent = shared_latent(key, 0.5, 2.0)
    key = jax.random.fold_in(key, 11)
    key_rows, key_noise = jax.random.split(key, 2)
    noise_part = jnp.clip(jax.random.normal(key_noise, (TOKENS, FF), jnp.float32), -4.0, 4.0)
    return mixed_rows(key_rows, latent, FF, noise_part).astype(jnp.bfloat16)


def draw_out_grads(key, part):
    latent = shared_latent(key, 0.5, 2.0)
    key = jax.random.fold_in(key, 23)
    key_rows, key_noise = jax.random.split(key, 2)
    noise_part = jnp.clip(jax.random.normal(key_noise, (TOKENS, D), jnp.float32), -4.0, 4.0)
    return mixed_rows(key_rows, latent, D, noise_part).astype(jnp.bfloat16)


def draw_lengths(key, part):
    key = jax.random.fold_in(key, 37)
    key_len, key_full = jax.random.split(key)
    drawn = jax.random.randint(key_len, (SEQS,), LEN // 4, LEN + 1)
    full_at = jax.random.randint(key_full, (), 0, SEQS)
    return jnp.where(jnp.arange(SEQS) == full_at, LEN, drawn).astype(jnp.int32)


def setup_inputs(seed: int = 0) -> dict:
    seeds = jax.random.split(jax.random.key(seed), 4)
    return {
        "activations": draw_activations(jax.random.fold_in(seeds[3], 71), 0),
        "out_grads": draw_out_grads(jax.random.fold_in(seeds[3], 71), 0),
        "lengths": draw_lengths(jax.random.fold_in(seeds[3], 71), 0),
    }


def reference(activations, out_grads, lengths):
    slots = jnp.arange(TOKENS, dtype=jnp.int32)
    position = slots % LEN
    seq_index = slots // LEN
    valid = position < lengths[seq_index]
    masked = jnp.where(valid[:, None], out_grads, jnp.zeros_like(out_grads))

    def one_row(block):
        begin_row = (block * LEN).astype(jnp.int32)
        act_rows = lax.dynamic_slice_in_dim(activations, begin_row, LEN, 0)
        grad_rows = lax.dynamic_slice_in_dim(masked, begin_row, LEN, 0)
        act_gram = jnp.dot(act_rows, activations.T, preferred_element_type=jnp.float32)
        grad_gram = jnp.dot(grad_rows, masked.T, preferred_element_type=jnp.float32)
        return (act_gram * grad_gram).reshape(LEN, SEQS, LEN).sum(axis=(0, 2))

    kernel = lax.map(one_row, jnp.arange(SEQS, dtype=jnp.int32))
    return kernel / float(LEN * FF * D)
```

```python
import jax
import jax.numpy as jnp
from jax import lax
from jax.experimental import pallas as pl
from jax.experimental.pallas import tpu as pltpu
from jax.sharding import PartitionSpec as P

FF = 28672
D = 8192
LEN = 384
SEQS = 16

MESH = pl.DeviceIdType.MESH
AH = FF // 32
GH = D // 32
WH = AH + GH
CH = 128
QR = CH // 4
UNITS = 37
SAMES = 13
LAG = 4
NT = (((1,), (1,)), ((), ()))


def device(h, y, c, x, l):
    return {"ex": (h * 4 + y) * 2 + c, "feat": x * 4 + l}


def bytes_wait(ref, sem):
    pltpu.make_async_copy(ref, ref, sem).wait()


def pick(index, values):
    out = values[-1]
    for i in range(len(values) - 2, -1, -1):
        out = jnp.where(index == i, values[i], out)
    return out


def body(act_ref, grad_ref, len_ref, out_ref, w, graw, xp, xq, rp, rq, sp2, sq2, rp2, rq2,
         zs, zr, zc, tb, in_sem, sib_s, sib_r, far_s, far_r, y_s, y_r, fw_s, fw_r, rf_s, rf_r,
         x1_s, x1_r, x2_s, x2_r, z_s, z_r, c_r, t_s, t_r):
    e = lax.axis_index("ex")
    f = lax.axis_index("feat")
    h, y, c = e // 8, (e // 2) % 4, e % 2
    x, l = f // 4, f % 4
    zz = h * 4 + l
    own = 4 + 2 * c
    up, down = (y + 1) % 4, (y + 3) % 4
    sgn = 1 - 2 * c
    qa, qb = ((x + 1) // 2) % 2, x // 2
    xa, xb = x + 1 - 2 * (x % 2), 3 - x
    c2 = jnp.where(y < 2, c, 1 - c)

    loads = []
    for half in range(2):
        loads.append(pltpu.make_async_copy(
            act_ref.at[:, pl.ds(half * AH, AH)], w.at[own + half, :, pl.ds(0, AH)],
            in_sem.at[half]))
    loads.append(pltpu.make_async_copy(grad_ref, graw, in_sem.at[2]))
    for ld in loads:
        ld.start()

    def other_side(t, k):
        o_shift = jnp.where(t == 0, 0, jnp.where(t == 1, 1, jnp.where(t == 2, 3, 4 - sgn)))
        y2 = jnp.where(t == 3, y + o_shift + 4 - (1 - 2 * k), y + o_shift) % 4
        t2 = jnp.where(t == 1, 2, jnp.where(t == 2, 1, t))
        return y2, t2

    kept = (c + h) % 2

    bar = pltpu.get_barrier_semaphore()

    def greet(dev):
        pl.semaphore_signal(bar, inc=1, device_id=dev, device_id_type=MESH)

    def plane(i):
        return device(h, i % 4, c, i // 4, l)

    def column(i):
        return device(i // 8, y, i % 2, x, (i // 2) % 4)

    in_plane, in_column = x * 4 + y, zz * 2 + c
    for d in range(1, 16):
        greet(plane((in_plane + d) % 16))
        greet(column((in_column + d) % 16))
    ysrc, _ = other_side(l, kept)
    for l2 in range(4):
        greet(device(1 - h, ysrc, kept, x, l2))

    for ld in loads:
        ld.wait()
    rows = lax.broadcasted_iota(jnp.int32, (LEN, GH), 0)
    valid = rows < len_ref[0]
    for half in range(2):
        g = graw[:, half * GH:(half + 1) * GH].astype(jnp.float32)
        w[own + half, :, AH:WH] = jnp.where(valid, g, 0.0).astype(jnp.bfloat16)
    pl.semaphore_wait(bar, 34)

    def start(src, dst, send, recv, dev):
        pltpu.make_async_remote_copy(src_ref=src, dst_ref=dst, send_sem=send, recv_sem=recv,
                                     device_id=dev, device_id_type=MESH).start()

    def chunk(j):
        return pl.ds(pl.multiple_of(j * CH, CH), CH)

    sibling = device(h, y, 1 - c, x, l)

    def send_far(j):
        start(w.at[own + 1 - h, chunk(j)], w.at[12, chunk(j)], far_s.at[j], far_r.at[j],
              device(1 - h, y, c, x, l))

    def send_near(j):
        start(w.at[pl.ds(own, 2), chunk(j)], w.at[pl.ds(8 + 2 * c, 2), chunk(j)],
              y_s.at[j, 0], y_r.at[j, 0], device(h, down, c, x, l))
        start(w.at[pl.ds(own, 2), chunk(j)], w.at[pl.ds(2 * c, 2), chunk(j)],
              y_s.at[j, 1], y_r.at[j, 1], device(h, up, c, x, l))

    for j in range(2):
        send_far(j)
        send_near(j)
    start(w.at[pl.ds(own, 2)], w.at[pl.ds(own, 2)], sib_s, sib_r, sibling)

    def arrive(j):
        for s in range(2):
            bytes_wait(w.at[pl.ds((8 if s == 0 else 0) + 2 * c, 2), chunk(j)], y_r.at[j, s])

        @pl.when(j < 1)
        def _():
            send_near(j + 2)

        for s in range(2):
            slot = pl.ds((8 if s == 0 else 0) + 2 * c, 2)
            start(w.at[slot, chunk(j)], w.at[slot, chunk(j)], fw_s.at[j, s], fw_r.at[j, s], sibling)
        bytes_wait(w.at[12, chunk(j)], far_r.at[j])

        @pl.when(j < 1)
        def _():
            send_far(j + 2)

        start(w.at[12, chunk(j)], w.at[13, chunk(j)], rf_s.at[j], rf_r.at[j],
              device(h, jnp.where(c == 0, down, up), c, x, l))
        for s in range(2):
            slot = pl.ds((8 if s == 0 else 0) + 2 * (1 - c), 2)
            bytes_wait(w.at[slot, chunk(j)], fw_r.at[j, s])

    def stage_of(p):
        j = jnp.where(p < 8, 0, jnp.where(p < 17, 1, 2))
        return j, jnp.where(p > 32, p - 33, p - pick(j, (4, 8, 15)))

    def corner(p):
        late = p > 34
        return (jnp.where(p < 17, p - 12, jnp.where(late, 0, (p - 17) // 2)),
                jnp.where(p < 17, 0, jnp.where(late, p - 34, 1 + (p - 19) % 2)))

    def in_stage(p):
        return ((p >= 4) & (p < 12)) | (p == 17) | (p == 18) | (p == 33) | (p == 34)

    def in_corner(p):
        return ((p >= 12) & (p < 17)) | ((p >= 19) & (p < 27)) | (p > 34)

    def cross_of(p):
        j, q = stage_of(p)
        v, u = corner(p)
        m = p - 27
        st, co = in_stage(p), in_corner(p)
        t = jnp.where(st, 0, jnp.where(co, (v + 1) // 2, 3))
        k = jnp.where(st, q - 2, jnp.where(co, (v + 1) % 2, m // 3))
        return t, k, jnp.where(st, j, jnp.where(co, u, m % 3))

    def is_cross(p):
        return (in_stage(p) & (stage_of(p)[1] >= 2)) | (in_corner(p) & (corner(p)[0] > 0)) | (
            (p > 26) & (p < 33))

    def same_of(p):
        j, q = stage_of(p)
        return jnp.where(p < 4, p, jnp.where(in_stage(p), 4 + 2 * j + q, 10 + corner(p)[1]))

    def unit_of_same(s):
        j, q = (s - 4) // 2, (s - 4) % 2
        return jnp.where(s < 4, s, jnp.where(s < 10, pick(j, (4, 8, 33)) + q,
                                             pick(s - 10, (12, 35, 36))))

    def multiply(p):
        cross = is_cross(p)
        j, q = stage_of(p)
        v, u = corner(p)
        t, k, part = cross_of(p)
        st, co = in_stage(p), in_corner(p)
        left = jnp.where(p < 2, own, jnp.where(p < 4, 4, jnp.where(st, own, 2 * c)))
        right = jnp.where(p < 2, own, jnp.where(p < 4, 6, jnp.where(st, 8 + 2 * q, 8 + 2 * c2)))
        o = 2 * (pick(t, (2, 4, 0, 4 * c)) + k) + h
        r = jnp.where(t == 3, 13, 12)
        left = jnp.where(cross, jnp.where(h == 0, o, r), left)
        right = jnp.where(cross, jnp.where(h == 0, r, o), right)
        row_wise = cross & (t == 0) & (h == 1)
        col = jnp.where(p == 2, c, jnp.where(p == 3, 2, jnp.where(st, j, p - 27) % 3))
        us = pick(u, (0, 1, 2))
        for b in range(3):
            ib = jnp.where(row_wise, j, b)
            jb = jnp.where(row_wise, b, col)
            ib = jnp.where(co, pick(us, ((0, 1, 1)[b], (0, 0, 1)[b], 2)), ib)
            jb = jnp.where(co, pick(us, ((1, 0, 1)[b], (0, 2, 2)[b], b)), jb)
            ib = jnp.where(p == 0, b, jnp.where(p == 1, (1, 2, 2)[b], ib))
            jb = jnp.where(p == 0, b, jnp.where(p == 1, (0, 0, 1)[b], jb))

            def gram(half, c0, c1):
                return lax.dot_general(w[left + half, chunk(ib), c0:c1], w[right + half, chunk(jb), c0:c1],
                                       NT, preferred_element_type=jnp.float32)

            def store(pa, qg):
                pa, qg = pa.astype(jnp.bfloat16), qg.astype(jnp.bfloat16)
                for a in range(2):
                    for bb in range(2):
                        sl = slice((2 * a + bb) * QR, (2 * a + bb + 1) * QR)
                        xp[p, a, bb, b] = pa[sl]
                        xq[p, bb, a, b] = qg[sl]

            @pl.when(cross)
            def _():
                store(gram(0, 0, AH), gram(0, AH, WH))

            @pl.when(jnp.logical_not(cross))
            def _():
                store(gram(0, 0, AH) + gram(1, 0, AH), gram(0, AH, WH) + gram(1, AH, WH))

        start(xp.at[p, 1 - qa], rp.at[p], x1_s.at[0], x1_r.at[p, 0], device(h, y, c, xa, l))
        start(xq.at[p, 1 - qb], rq.at[p], x1_s.at[1], x1_r.at[p, 1], device(h, y, c, xb, l))

    def f32(v):
        return v.astype(jnp.float32)

    def exchange(p):
        bytes_wait(rp.at[p], x1_r.at[p, 0])
        sp2[p] = (f32(xp[p, qa, 1 - qb]) + f32(rp[p, 1 - qb])).astype(jnp.bfloat16)
        start(sp2.at[p], rp2.at[p], x2_s.at[0], x2_r.at[p, 0], device(h, y, c, xb, l))
        bytes_wait(rq.at[p], x1_r.at[p, 1])
        sq2[p] = (f32(xq[p, qb, 1 - qa]) + f32(rq[p, 1 - qa])).astype(jnp.bfloat16)
        start(sq2.at[p], rq2.at[p], x2_s.at[1], x2_r.at[p, 1], device(h, y, c, xa, l))

    def finish(p):
        bytes_wait(rp2.at[p], x2_r.at[p, 0])
        zs[p, :, :, 0:CH] = (f32(xp[p, qa, qb]) + f32(rp[p, qb]) + f32(rp2[p])).astype(jnp.bfloat16)
        bytes_wait(rq2.at[p], x2_r.at[p, 1])
        zs[p, :, :, CH:2 * CH] = (f32(xq[p, qb, qa]) + f32(rq[p, qa]) + f32(rq2[p])).astype(jnp.bfloat16)
        cross = is_cross(p)
        s = same_of(p)
        t, k, part = cross_of(p)
        mine = k == kept

        @pl.when(jnp.logical_not(cross) & (s % 4 != l))
        def _():
            o = s % 4
            start(zs.at[p], zr.at[s, (l - o + 3) % 4], z_s.at[p], z_r.at[s],
                  device(h, y, c, x, o))

        @pl.when(cross & mine & (t == l))
        def _():
            zc[zz, part] = zs[p]

        @pl.when(cross & jnp.logical_not(mine & (t == l)))
        def _():
            y2, t2 = other_side(t, k)
            dev = device(jnp.where(mine, h, 1 - h), jnp.where(mine, y, y2),
                         jnp.where(mine, c, k), x, jnp.where(mine, t, t2))
            start(zs.at[p], zc.at[zz, part], z_s.at[p], c_r, dev)

    row_id = lax.broadcasted_iota(jnp.int32, (SEQS, 128), 0)
    col_id = lax.broadcasted_iota(jnp.int32, (SEQS, 128), 1)

    def put(value, b, s):
        hit = ((row_id == b) & (col_id == s)) | ((row_id == s) & (col_id == b))
        return jnp.where(hit, value, 0.0)

    def seq(hh, yy, cc):
        return (hh * 4 + yy) * 2 + cc

    def keep_same(s):
        p = unit_of_same(s)

        @pl.when(s % 4 == l)
        def _():
            bytes_wait(zr.at[s], z_r.at[s])
            total = f32(zs[p])
            for d in range(3):
                total = total + f32(zr[s, d])
            value = jnp.sum(total[:, :, 0:CH] * total[:, :, CH:2 * CH])
            value = value * jnp.where(s == 1, 2.0, jnp.where(s == 3, 0.5, 1.0))
            b = jnp.where(s < 2, e, jnp.where(s < 4, seq(h, y, 0), jnp.where(
                s < 10, e, seq(h, down, c))))
            b2 = jnp.where(s < 2, e, jnp.where(s < 4, seq(h, y, 1), jnp.where(
                s < 10, seq(h, up, s % 2), seq(h, up, c2))))
            tb[0, in_plane] = tb[0, in_plane] + put(value, b, b2)

    tb[0, in_plane] = jnp.zeros((SEQS, 128), jnp.float32)

    @pl.loop(0, UNITS)
    def _(p):
        @pl.when(p == 2)
        def _():
            bytes_wait(w.at[pl.ds(own, 2)], sib_r)

        @pl.when(p == 4)
        def _():
            @pl.loop(0, 4)
            def _(i):
                exchange(p - 4 + i)

            @pl.loop(0, 4)
            def _(i):
                finish(p - 4 + i)

        @pl.when((p == 4) | (p == 8) | (p == 17))
        def _():
            arrive(stage_of(p)[0])

        @pl.when(p == 27)
        def _():
            for j in range(3):
                bytes_wait(w.at[13, chunk(j)], rf_r.at[j])

        multiply(p)

        @pl.when(p >= 4 + LAG)
        def _():
            exchange(p - LAG)

        @pl.when(p >= 4 + 2 * LAG)
        def _():
            finish(p - 2 * LAG)

        @pl.when(p == UNITS - 3)
        def _():
            @pl.loop(0, 8)
            def _(s):
                keep_same(s)

    @pl.loop(UNITS, UNITS + 2 * LAG)
    def _(p):
        @pl.when(p < UNITS + LAG)
        def _():
            exchange(p - LAG)

        finish(p - 2 * LAG)

    bytes_wait(zc.at[pl.ds(0, 7)], c_r)
    o_y = jnp.where(l == 0, y, jnp.where(l == 1, up, jnp.where(l == 2, down, (y + 4 - sgn) % 4)))
    r_y = jnp.where(l == 3, (y + 4 + sgn) % 4, y)

    def cross_block(i, acc):
        a, b = i // 3, i % 3
        a2, b2 = jnp.where(l == 0, b, a), jnp.where(l == 0, a, b)
        total = jnp.zeros((QR, 2 * CH), jnp.float32)
        for src in range(4):
            total = total + f32(zc[src, a2, b2])
        for src in range(4, 8):
            total = total + f32(zc[src, a, b])
        return acc + total[:, 0:CH] * total[:, CH:2 * CH]

    acc = lax.fori_loop(0, 9, cross_block, jnp.zeros((QR, CH), jnp.float32))
    tb[0, in_plane] = tb[0, in_plane] + put(
        jnp.sum(acc), seq(h, o_y, kept), seq(1 - h, r_y, c))

    @pl.loop(8, SAMES)
    def _(s):
        keep_same(s)

    def add_up(s, me, dev_of):
        for d in range(1, 16):
            start(tb.at[s, me], tb.at[s, me], t_s.at[s], t_r.at[s], dev_of((me + d) % 16))
        bytes_wait(tb.at[s, pl.ds(0, 15)], t_r.at[s])
        total = tb[s, 0]
        for d in range(1, 16):
            total = total + tb[s, d]
        return total

    tb[1, in_column] = add_up(0, in_plane, plane)
    total = add_up(1, in_column, column)
    line = jnp.sum(jnp.where(row_id == e, total, 0.0), axis=0, keepdims=True)
    out_ref[...] = line[:, 0:SEQS] / float(LEN * FF * D)

    bytes_wait(w.at[pl.ds(0, 2)], sib_s)
    for j in range(3):
        bytes_wait(w.at[0, chunk(j)], far_s.at[j])
        bytes_wait(w.at[0, chunk(j)], rf_s.at[j])
        for s in range(2):
            bytes_wait(w.at[pl.ds(0, 2), chunk(j)], y_s.at[j, s])
            bytes_wait(w.at[pl.ds(0, 2), chunk(j)], fw_s.at[j, s])
    for s in range(2):
        bytes_wait(tb.at[s, pl.ds(0, 15)], t_s.at[s])
    bytes_wait(rp, x1_s.at[0])
    bytes_wait(rq, x1_s.at[1])
    bytes_wait(rp2, x2_s.at[0])
    bytes_wait(rq2, x2_s.at[1])

    @pl.loop(0, UNITS)
    def _(p):
        t, k, _ = cross_of(p)
        here = jnp.where(is_cross(p), (k == kept) & (t == l), same_of(p) % 4 == l)

        @pl.when(jnp.logical_not(here))
        def _():
            bytes_wait(zs.at[p], z_s.at[p])


def per_device(activations, out_grads, lengths):
    bf, dma = jnp.bfloat16, pltpu.SemaphoreType.DMA
    return pl.pallas_call(
        body,
        out_shape=jax.ShapeDtypeStruct((1, SEQS), jnp.float32),
        in_specs=[pl.BlockSpec(memory_space=pl.ANY), pl.BlockSpec(memory_space=pl.ANY),
                  pl.BlockSpec(memory_space=pltpu.SMEM)],
        out_specs=pl.BlockSpec(memory_space=pltpu.VMEM),
        scratch_shapes=[
            pltpu.VMEM((14, LEN, WH), bf),
            pltpu.VMEM((LEN, 2 * GH), bf),
            pltpu.VMEM((UNITS, 2, 2, 3, QR, CH), bf),
            pltpu.VMEM((UNITS, 2, 2, 3, QR, CH), bf),
            pltpu.VMEM((UNITS, 2, 3, QR, CH), bf),
            pltpu.VMEM((UNITS, 2, 3, QR, CH), bf),
            pltpu.VMEM((UNITS, 3, QR, CH), bf),
            pltpu.VMEM((UNITS, 3, QR, CH), bf),
            pltpu.VMEM((UNITS, 3, QR, CH), bf),
            pltpu.VMEM((UNITS, 3, QR, CH), bf),
            pltpu.VMEM((UNITS, 3, QR, 2 * CH), bf),
            pltpu.VMEM((SAMES, 3, 3, QR, 2 * CH), bf),
            pltpu.VMEM((8, 3, 3, QR, 2 * CH), bf),
            pltpu.VMEM((2, 16, SEQS, 128), jnp.float32),
            dma((3,)), dma, dma, dma((3,)), dma((3,)),
            dma((3, 2)), dma((3, 2)), dma((3, 2)), dma((3, 2)), dma((3,)), dma((3,)),
            dma((2,)), dma((UNITS, 2)), dma((2,)), dma((UNITS, 2)), dma((UNITS,)), dma((SAMES,)), dma,
            dma((2,)), dma((2,)),
        ],
        compiler_params=pltpu.CompilerParams(
            collective_id=0, has_side_effects=True, vmem_limit_bytes=56 << 20),
        name="ghost_kernel",
    )(activations, out_grads, lengths)


def solution(mesh):
    placed = (P("ex", "feat"), P("ex", "feat"), P("ex"))
    return jax.shard_map(
        per_device, mesh=mesh, in_specs=placed, out_specs=P("ex", None), check_vma=False
    )
```

```python
import jax
import jax.numpy as jnp
from jax import lax
from jax.experimental import pallas as pl
from jax.experimental.pallas import tpu as pltpu
from jax.sharding import PartitionSpec as P

FF = 28672
D = 8192
LEN = 384
SEQS = 16

MESH = pl.DeviceIdType.MESH
AH = FF // 32
GH = D // 32
WH = AH + GH
CH = 128
QR = CH // 4
UNITS = 37
SAMES = 13
LAG = 3
NT = (((1,), (1,)), ((), ()))


def device(h, y, c, x, l):
    return {"ex": (h * 4 + y) * 2 + c, "feat": x * 4 + l}


def bytes_wait(ref, sem):
    pltpu.make_async_copy(ref, ref, sem).wait()


def pick(index, values):
    out = values[-1]
    for i in range(len(values) - 2, -1, -1):
        out = jnp.where(index == i, values[i], out)
    return out


def body(act_ref, grad_ref, len_ref, out_ref, w, graw, xp, xq, rp, rq, sp2, sq2, rp2, rq2,
         zs, zr, zc, tb, in_sem, sib_s, sib_r, far_s, far_r, y_s, y_r, fw_s, fw_r, rf_s, rf_r,
         x1_s, x1_r, x2_s, x2_r, z_s, z_r, c_r, t_s, t_r):
    e = lax.axis_index("ex")
    f = lax.axis_index("feat")
    h, y, c = e // 8, (e // 2) % 4, e % 2
    x, l = f // 4, f % 4
    zz = h * 4 + l
    own = 4 + 2 * c
    up, down = (y + 1) % 4, (y + 3) % 4
    sgn = 1 - 2 * c
    qa, qb = ((x + 1) // 2) % 2, x // 2
    xa, xb = x + 1 - 2 * (x % 2), 3 - x
    c2 = jnp.where(y < 2, c, 1 - c)

    loads = []
    for half in range(2):
        loads.append(pltpu.make_async_copy(
            act_ref.at[:, pl.ds(half * AH, AH)], w.at[own + half, :, pl.ds(0, AH)],
            in_sem.at[half]))
    loads.append(pltpu.make_async_copy(grad_ref, graw, in_sem.at[2]))
    for ld in loads:
        ld.start()

    def other_side(t, k):
        o_shift = jnp.where(t == 0, 0, jnp.where(t == 1, 1, jnp.where(t == 2, 3, 4 - sgn)))
        y2 = jnp.where(t == 3, y + o_shift + 4 - (1 - 2 * k), y + o_shift) % 4
        t2 = jnp.where(t == 1, 2, jnp.where(t == 2, 1, t))
        return y2, t2

    kept = (c + h) % 2

    bar = pltpu.get_barrier_semaphore()

    def greet(dev):
        pl.semaphore_signal(bar, inc=1, device_id=dev, device_id_type=MESH)

    def plane(i):
        return device(h, i % 4, c, i // 4, l)

    def column(i):
        return device(i // 8, y, i % 2, x, (i // 2) % 4)

    in_plane, in_column = x * 4 + y, zz * 2 + c
    for d in range(1, 16):
        greet(plane((in_plane + d) % 16))
        greet(column((in_column + d) % 16))
    ysrc, _ = other_side(l, kept)
    for l2 in range(4):
        greet(device(1 - h, ysrc, kept, x, l2))

    for ld in loads:
        ld.wait()
    rows = lax.broadcasted_iota(jnp.int32, (LEN, GH), 0)
    valid = rows < len_ref[0]
    for half in range(2):
        g = graw[:, half * GH:(half + 1) * GH].astype(jnp.float32)
        w[own + half, :, AH:WH] = jnp.where(valid, g, 0.0).astype(jnp.bfloat16)
    pl.semaphore_wait(bar, 34)

    def start(src, dst, send, recv, dev):
        pltpu.make_async_remote_copy(src_ref=src, dst_ref=dst, send_sem=send, recv_sem=recv,
                                     device_id=dev, device_id_type=MESH).start()

    def chunk(j):
        return pl.ds(pl.multiple_of(j * CH, CH), CH)

    sibling = device(h, y, 1 - c, x, l)

    def send_far(j):
        start(w.at[own + 1 - h, chunk(j)], w.at[12, chunk(j)], far_s.at[j], far_r.at[j],
              device(1 - h, y, c, x, l))

    def send_near(j):
        start(w.at[pl.ds(own, 2), chunk(j)], w.at[pl.ds(8 + 2 * c, 2), chunk(j)],
              y_s.at[j, 0], y_r.at[j, 0], device(h, down, c, x, l))
        start(w.at[pl.ds(own, 2), chunk(j)], w.at[pl.ds(2 * c, 2), chunk(j)],
              y_s.at[j, 1], y_r.at[j, 1], device(h, up, c, x, l))

    for j in range(2):
        send_far(j)
        send_near(j)
    start(w.at[pl.ds(own, 2)], w.at[pl.ds(own, 2)], sib_s, sib_r, sibling)

    def arrive(j):
        for s in range(2):
            bytes_wait(w.at[pl.ds((8 if s == 0 else 0) + 2 * c, 2), chunk(j)], y_r.at[j, s])

        @pl.when(j < 1)
        def _():
            send_near(j + 2)

        for s in range(2):
            slot = pl.ds((8 if s == 0 else 0) + 2 * c, 2)
            start(w.at[slot, chunk(j)], w.at[slot, chunk(j)], fw_s.at[j, s], fw_r.at[j, s], sibling)
        bytes_wait(w.at[12, chunk(j)], far_r.at[j])

        @pl.when(j < 1)
        def _():
            send_far(j + 2)

        start(w.at[12, chunk(j)], w.at[13, chunk(j)], rf_s.at[j], rf_r.at[j],
              device(h, jnp.where(c == 0, down, up), c, x, l))
        for s in range(2):
            slot = pl.ds((8 if s == 0 else 0) + 2 * (1 - c), 2)
            bytes_wait(w.at[slot, chunk(j)], fw_r.at[j, s])

    def stage_of(p):
        j = jnp.where(p < 8, 0, jnp.where(p < 17, 1, 2))
        return j, jnp.where(p > 32, p - 33, p - pick(j, (4, 8, 15)))

    def corner(p):
        late = p > 34
        return (jnp.where(p < 17, p - 12, jnp.where(late, 0, (p - 17) // 2)),
                jnp.where(p < 17, 0, jnp.where(late, p - 34, 1 + (p - 19) % 2)))

    def in_stage(p):
        return ((p >= 4) & (p < 12)) | (p == 17) | (p == 18) | (p == 33) | (p == 34)

    def in_corner(p):
        return ((p >= 12) & (p < 17)) | ((p >= 19) & (p < 27)) | (p > 34)

    def cross_of(p):
        j, q = stage_of(p)
        v, u = corner(p)
        m = p - 27
        st, co = in_stage(p), in_corner(p)
        t = jnp.where(st, 0, jnp.where(co, (v + 1) // 2, 3))
        k = jnp.where(st, q - 2, jnp.where(co, (v + 1) % 2, m // 3))
        return t, k, jnp.where(st, j, jnp.where(co, u, m % 3))

    def is_cross(p):
        return (in_stage(p) & (stage_of(p)[1] >= 2)) | (in_corner(p) & (corner(p)[0] > 0)) | (
            (p > 26) & (p < 33))

    def same_of(p):
        j, q = stage_of(p)
        return jnp.where(p < 4, p, jnp.where(in_stage(p), 4 + 2 * j + q, 10 + corner(p)[1]))

    def unit_of_same(s):
        j, q = (s - 4) // 2, (s - 4) % 2
        return jnp.where(s < 4, s, jnp.where(s < 10, pick(j, (4, 8, 33)) + q,
                                             pick(s - 10, (12, 35, 36))))

    def multiply(p):
        cross = is_cross(p)
        j, q = stage_of(p)
        v, u = corner(p)
        t, k, part = cross_of(p)
        st, co = in_stage(p), in_corner(p)
        left = jnp.where(p < 2, own, jnp.where(p < 4, 4, jnp.where(st, own, 2 * c)))
        right = jnp.where(p < 2, own, jnp.where(p < 4, 6, jnp.where(st, 8 + 2 * q, 8 + 2 * c2)))
        o = 2 * (pick(t, (2, 4, 0, 4 * c)) + k) + h
        r = jnp.where(t == 3, 13, 12)
        left = jnp.where(cross, jnp.where(h == 0, o, r), left)
        right = jnp.where(cross, jnp.where(h == 0, r, o), right)
        row_wise = (cross & (t == 0) & (h == 1)) | (co & (u == 2))
        row = jnp.where(co, 2, j)
        col_wise = jnp.logical_not(row_wise | co | (p < 2))
        col = jnp.where(p == 2, c, jnp.where(p == 3, 2, jnp.where(st, j, p - 27) % 3))

        def gram(rows, cols, c0, c1, halves):
            total = None
            for half in range(halves):
                part = lax.dot_general(w[left + half, rows, c0:c1], w[right + half, cols, c0:c1],
                                       NT, preferred_element_type=jnp.float32)
                total = part if total is None else total + part
            return total.astype(jnp.bfloat16)

        def store(b, pa, qg):
            for a in range(2):
                for bb in range(2):
                    sl = slice((2 * a + bb) * QR, (2 * a + bb + 1) * QR)
                    xp[p, a, bb, b] = pa[sl]
                    xq[p, bb, a, b] = qg[sl]

        for halves in (1, 2):
            mine = cross if halves == 1 else jnp.logical_not(cross)
            whole = slice(None)

            @pl.when(mine & col_wise)
            def _():
                pa = gram(whole, chunk(col), 0, AH, halves)
                qg = gram(whole, chunk(col), AH, WH, halves)
                for b in range(3):
                    sl = slice(b * CH, (b + 1) * CH)
                    store(b, pa[sl], qg[sl])

            @pl.when(mine & row_wise)
            def _():
                pa = gram(chunk(row), whole, 0, AH, halves)
                qg = gram(chunk(row), whole, AH, WH, halves)
                for b in range(3):
                    sl = slice(b * CH, (b + 1) * CH)
                    store(b, pa[:, sl], qg[:, sl])

            @pl.when(mine & jnp.logical_not(row_wise | col_wise))
            def _():
                for b in range(3):
                    ib = jnp.where(u == 0, (0, 1, 1)[b], (0, 0, 1)[b])
                    jb = jnp.where(u == 0, (1, 0, 1)[b], (0, 2, 2)[b])
                    ib = jnp.where(p == 0, b, jnp.where(p == 1, (1, 2, 2)[b], ib))
                    jb = jnp.where(p == 0, b, jnp.where(p == 1, (0, 0, 1)[b], jb))
                    store(b, gram(chunk(ib), chunk(jb), 0, AH, halves),
                          gram(chunk(ib), chunk(jb), AH, WH, halves))

        start(xp.at[p, 1 - qa], rp.at[p], x1_s.at[0], x1_r.at[p, 0], device(h, y, c, xa, l))
        start(xq.at[p, 1 - qb], rq.at[p], x1_s.at[1], x1_r.at[p, 1], device(h, y, c, xb, l))

    def f32(v):
        return v.astype(jnp.float32)

    def exchange(p):
        bytes_wait(rp.at[p], x1_r.at[p, 0])
        sp2[p] = (f32(xp[p, qa, 1 - qb]) + f32(rp[p, 1 - qb])).astype(jnp.bfloat16)
        start(sp2.at[p], rp2.at[p], x2_s.at[0], x2_r.at[p, 0], device(h, y, c, xb, l))
        bytes_wait(rq.at[p], x1_r.at[p, 1])
        sq2[p] = (f32(xq[p, qb, 1 - qa]) + f32(rq[p, 1 - qa])).astype(jnp.bfloat16)
        start(sq2.at[p], rq2.at[p], x2_s.at[1], x2_r.at[p, 1], device(h, y, c, xa, l))

    def finish(p):
        bytes_wait(rp2.at[p], x2_r.at[p, 0])
        zs[p, :, :, 0:CH] = (f32(xp[p, qa, qb]) + f32(rp[p, qb]) + f32(rp2[p])).astype(jnp.bfloat16)
        bytes_wait(rq2.at[p], x2_r.at[p, 1])
        zs[p, :, :, CH:2 * CH] = (f32(xq[p, qb, qa]) + f32(rq[p, qa]) + f32(rq2[p])).astype(jnp.bfloat16)
        cross = is_cross(p)
        s = same_of(p)
        t, k, part = cross_of(p)
        mine = k == kept

        @pl.when(jnp.logical_not(cross) & (s % 4 != l))
        def _():
            o = s % 4
            start(zs.at[p], zr.at[s, (l - o + 3) % 4], z_s.at[p], z_r.at[s],
                  device(h, y, c, x, o))

        @pl.when(cross & mine & (t == l))
        def _():
            zc[zz, part] = zs[p]

        @pl.when(cross & jnp.logical_not(mine & (t == l)))
        def _():
            y2, t2 = other_side(t, k)
            dev = device(jnp.where(mine, h, 1 - h), jnp.where(mine, y, y2),
                         jnp.where(mine, c, k), x, jnp.where(mine, t, t2))
            start(zs.at[p], zc.at[zz, part], z_s.at[p], c_r, dev)

    row_id = lax.broadcasted_iota(jnp.int32, (SEQS, 128), 0)
    col_id = lax.broadcasted_iota(jnp.int32, (SEQS, 128), 1)

    def put(value, b, s):
        hit = ((row_id == b) & (col_id == s)) | ((row_id == s) & (col_id == b))
        return jnp.where(hit, value, 0.0)

    def seq(hh, yy, cc):
        return (hh * 4 + yy) * 2 + cc

    def keep_same(s):
        p = unit_of_same(s)

        @pl.when(s % 4 == l)
        def _():
            bytes_wait(zr.at[s], z_r.at[s])
            total = f32(zs[p])
            for d in range(3):
                total = total + f32(zr[s, d])
            value = jnp.sum(total[:, :, 0:CH] * total[:, :, CH:2 * CH])
            value = value * jnp.where(s == 1, 2.0, jnp.where(s == 3, 0.5, 1.0))
            b = jnp.where(s < 2, e, jnp.where(s < 4, seq(h, y, 0), jnp.where(
                s < 10, e, seq(h, down, c))))
            b2 = jnp.where(s < 2, e, jnp.where(s < 4, seq(h, y, 1), jnp.where(
                s < 10, seq(h, up, s % 2), seq(h, up, c2))))
            tb[0, in_plane] = tb[0, in_plane] + put(value, b, b2)

    tb[0, in_plane] = jnp.zeros((SEQS, 128), jnp.float32)

    @pl.loop(0, UNITS)
    def _(p):
        @pl.when(p == 2)
        def _():
            bytes_wait(w.at[pl.ds(own, 2)], sib_r)

        @pl.when(p == 4)
        def _():
            @pl.loop(0, 4)
            def _(i):
                exchange(p - 4 + i)

            @pl.loop(0, 4)
            def _(i):
                finish(p - 4 + i)

        @pl.when((p == 4) | (p == 8) | (p == 17))
        def _():
            arrive(stage_of(p)[0])

        @pl.when(p == 27)
        def _():
            for j in range(3):
                bytes_wait(w.at[13, chunk(j)], rf_r.at[j])

        multiply(p)

        @pl.when(p >= 4 + LAG)
        def _():
            exchange(p - LAG)

        @pl.when(p >= 4 + 2 * LAG)
        def _():
            finish(p - 2 * LAG)

        @pl.when(p == UNITS - 3)
        def _():
            @pl.loop(0, 8)
            def _(s):
                keep_same(s)

    @pl.loop(UNITS, UNITS + 2 * LAG)
    def _(p):
        @pl.when(p < UNITS + LAG)
        def _():
            exchange(p - LAG)

        finish(p - 2 * LAG)

    bytes_wait(zc.at[pl.ds(0, 7)], c_r)
    o_y = jnp.where(l == 0, y, jnp.where(l == 1, up, jnp.where(l == 2, down, (y + 4 - sgn) % 4)))
    r_y = jnp.where(l == 3, (y + 4 + sgn) % 4, y)

    def cross_block(i, acc):
        a, b = i // 3, i % 3
        a2, b2 = jnp.where(l == 0, b, a), jnp.where(l == 0, a, b)
        total = jnp.zeros((QR, 2 * CH), jnp.float32)
        for src in range(4):
            total = total + f32(zc[src, a2, b2])
        for src in range(4, 8):
            total = total + f32(zc[src, a, b])
        return acc + total[:, 0:CH] * total[:, CH:2 * CH]

    acc = lax.fori_loop(0, 9, cross_block, jnp.zeros((QR, CH), jnp.float32))
    tb[0, in_plane] = tb[0, in_plane] + put(
        jnp.sum(acc), seq(h, o_y, kept), seq(1 - h, r_y, c))

    @pl.loop(8, SAMES)
    def _(s):
        keep_same(s)

    def add_up(s, me, dev_of):
        for d in range(1, 16):
            start(tb.at[s, me], tb.at[s, me], t_s.at[s], t_r.at[s], dev_of((me + d) % 16))
        bytes_wait(tb.at[s, pl.ds(0, 15)], t_r.at[s])
        total = tb[s, 0]
        for d in range(1, 16):
            total = total + tb[s, d]
        return total

    tb[1, in_column] = add_up(0, in_plane, plane)
    total = add_up(1, in_column, column)
    line = jnp.sum(jnp.where(row_id == e, total, 0.0), axis=0, keepdims=True)
    out_ref[...] = line[:, 0:SEQS] / float(LEN * FF * D)

    bytes_wait(w.at[pl.ds(0, 2)], sib_s)
    for j in range(3):
        bytes_wait(w.at[0, chunk(j)], far_s.at[j])
        bytes_wait(w.at[0, chunk(j)], rf_s.at[j])
        for s in range(2):
            bytes_wait(w.at[pl.ds(0, 2), chunk(j)], y_s.at[j, s])
            bytes_wait(w.at[pl.ds(0, 2), chunk(j)], fw_s.at[j, s])
    for s in range(2):
        bytes_wait(tb.at[s, pl.ds(0, 15)], t_s.at[s])
    bytes_wait(rp, x1_s.at[0])
    bytes_wait(rq, x1_s.at[1])
    bytes_wait(rp2, x2_s.at[0])
    bytes_wait(rq2, x2_s.at[1])

    @pl.loop(0, UNITS)
    def _(p):
        t, k, _ = cross_of(p)
        here = jnp.where(is_cross(p), (k == kept) & (t == l), same_of(p) % 4 == l)

        @pl.when(jnp.logical_not(here))
        def _():
            bytes_wait(zs.at[p], z_s.at[p])


def per_device(activations, out_grads, lengths):
    bf, dma = jnp.bfloat16, pltpu.SemaphoreType.DMA
    return pl.pallas_call(
        body,
        out_shape=jax.ShapeDtypeStruct((1, SEQS), jnp.float32),
        in_specs=[pl.BlockSpec(memory_space=pl.ANY), pl.BlockSpec(memory_space=pl.ANY),
                  pl.BlockSpec(memory_space=pltpu.SMEM)],
        out_specs=pl.BlockSpec(memory_space=pltpu.VMEM),
        scratch_shapes=[
            pltpu.VMEM((14, LEN, WH), bf),
            pltpu.VMEM((LEN, 2 * GH), bf),
            pltpu.VMEM((UNITS, 2, 2, 3, QR, CH), bf),
            pltpu.VMEM((UNITS, 2, 2, 3, QR, CH), bf),
            pltpu.VMEM((UNITS, 2, 3, QR, CH), bf),
            pltpu.VMEM((UNITS, 2, 3, QR, CH), bf),
            pltpu.VMEM((UNITS, 3, QR, CH), bf),
            pltpu.VMEM((UNITS, 3, QR, CH), bf),
            pltpu.VMEM((UNITS, 3, QR, CH), bf),
            pltpu.VMEM((UNITS, 3, QR, CH), bf),
            pltpu.VMEM((UNITS, 3, QR, 2 * CH), bf),
            pltpu.VMEM((SAMES, 3, 3, QR, 2 * CH), bf),
            pltpu.VMEM((8, 3, 3, QR, 2 * CH), bf),
            pltpu.VMEM((2, 16, SEQS, 128), jnp.float32),
            dma((3,)), dma, dma, dma((3,)), dma((3,)),
            dma((3, 2)), dma((3, 2)), dma((3, 2)), dma((3, 2)), dma((3,)), dma((3,)),
            dma((2,)), dma((UNITS, 2)), dma((2,)), dma((UNITS, 2)), dma((UNITS,)), dma((SAMES,)), dma,
            dma((2,)), dma((2,)),
        ],
        compiler_params=pltpu.CompilerParams(
            collective_id=0, has_side_effects=True, vmem_limit_bytes=56 << 20),
        name="ghost_kernel",
    )(activations, out_grads, lengths)


def solution(mesh):
    placed = (P("ex", "feat"), P("ex", "feat"), P("ex"))
    return jax.shard_map(
        per_device, mesh=mesh, in_specs=placed, out_specs=P("ex", None), check_vma=False
    )
```

```python
import jax
import jax.numpy as jnp
from jax import lax
from jax.experimental import pallas as pl
from jax.experimental.pallas import tpu as pltpu
from jax.sharding import PartitionSpec as P

FF = 28672
D = 8192
LEN = 384
SEQS = 16

MESH = pl.DeviceIdType.MESH
AH = FF // 32
GH = D // 32
WH = AH + GH
CH = 128
QR = CH // 4
UNITS = 37
SAMES = 13
LAG = 3
NT = (((1,), (1,)), ((), ()))


def device(h, y, c, x, l):
    return {"ex": (h * 4 + y) * 2 + c, "feat": x * 4 + l}


def bytes_wait(ref, sem):
    pltpu.make_async_copy(ref, ref, sem).wait()


def pick(index, values):
    out = values[-1]
    for i in range(len(values) - 2, -1, -1):
        out = jnp.where(index == i, values[i], out)
    return out


def body(act_ref, grad_ref, len_ref, out_ref, w, graw, xp, xq, rp, rq, sp2, sq2, rp2, rq2,
         zs, zr, zc, tb, in_sem, sib_s, sib_r, far_s, far_r, y_s, y_r, fw_s, fw_r, rf_s, rf_r,
         x1_s, x1_r, x2_s, x2_r, z_s, z_r, c_r, t_s, t_r):
    e = lax.axis_index("ex")
    f = lax.axis_index("feat")
    h, y, c = e // 8, (e // 2) % 4, e % 2
    x, l = f // 4, f % 4
    zz = h * 4 + l
    own = 4 + 2 * c
    up, down = (y + 1) % 4, (y + 3) % 4
    sgn = 1 - 2 * c
    qa, qb = ((x + 1) // 2) % 2, x // 2
    xa, xb = x + 1 - 2 * (x % 2), 3 - x
    c2 = jnp.where(y < 2, c, 1 - c)

    loads = []
    for half in range(2):
        loads.append(pltpu.make_async_copy(
            act_ref.at[:, pl.ds(half * AH, AH)], w.at[own + half, :, pl.ds(0, AH)],
            in_sem.at[half]))
    loads.append(pltpu.make_async_copy(grad_ref, graw, in_sem.at[2]))
    for ld in loads:
        ld.start()

    def other_side(t, k):
        o_shift = jnp.where(t == 0, 0, jnp.where(t == 1, 1, jnp.where(t == 2, 3, 4 - sgn)))
        y2 = jnp.where(t == 3, y + o_shift + 4 - (1 - 2 * k), y + o_shift) % 4
        t2 = jnp.where(t == 1, 2, jnp.where(t == 2, 1, t))
        return y2, t2

    kept = (c + h) % 2

    bar = pltpu.get_barrier_semaphore()

    def greet(dev):
        pl.semaphore_signal(bar, inc=1, device_id=dev, device_id_type=MESH)

    def plane(i):
        return device(h, i % 4, c, i // 4, l)

    def column(i):
        return device(i // 8, y, i % 2, x, (i // 2) % 4)

    in_plane, in_column = x * 4 + y, zz * 2 + c
    for d in range(1, 16):
        greet(plane((in_plane + d) % 16))
        greet(column((in_column + d) % 16))
    ysrc, _ = other_side(l, kept)
    for l2 in range(4):
        greet(device(1 - h, ysrc, kept, x, l2))

    for ld in loads:
        ld.wait()
    rows = lax.broadcasted_iota(jnp.int32, (LEN, GH), 0)
    valid = rows < len_ref[0]
    for half in range(2):
        g = graw[:, half * GH:(half + 1) * GH].astype(jnp.float32)
        w[own + half, :, AH:WH] = jnp.where(valid, g, 0.0).astype(jnp.bfloat16)
    pl.semaphore_wait(bar, 34)

    def start(src, dst, send, recv, dev):
        pltpu.make_async_remote_copy(src_ref=src, dst_ref=dst, send_sem=send, recv_sem=recv,
                                     device_id=dev, device_id_type=MESH).start()

    def chunk(j):
        return pl.ds(pl.multiple_of(j * CH, CH), CH)

    sibling = device(h, y, 1 - c, x, l)

    def send_far(j):
        start(w.at[own + 1 - h, chunk(j)], w.at[12, chunk(j)], far_s.at[j], far_r.at[j],
              device(1 - h, y, c, x, l))

    def send_near(j):
        start(w.at[pl.ds(own, 2), chunk(j)], w.at[pl.ds(8 + 2 * c, 2), chunk(j)],
              y_s.at[j, 0], y_r.at[j, 0], device(h, down, c, x, l))
        start(w.at[pl.ds(own, 2), chunk(j)], w.at[pl.ds(2 * c, 2), chunk(j)],
              y_s.at[j, 1], y_r.at[j, 1], device(h, up, c, x, l))

    for j in range(2):
        send_far(j)
        send_near(j)
    start(w.at[pl.ds(own, 2)], w.at[pl.ds(own, 2)], sib_s, sib_r, sibling)

    def arrive(j):
        for s in range(2):
            bytes_wait(w.at[pl.ds((8 if s == 0 else 0) + 2 * c, 2), chunk(j)], y_r.at[j, s])

        @pl.when(j < 1)
        def _():
            send_near(j + 2)

        for s in range(2):
            slot = pl.ds((8 if s == 0 else 0) + 2 * c, 2)
            start(w.at[slot, chunk(j)], w.at[slot, chunk(j)], fw_s.at[j, s], fw_r.at[j, s], sibling)
        bytes_wait(w.at[12, chunk(j)], far_r.at[j])

        @pl.when(j < 1)
        def _():
            send_far(j + 2)

        start(w.at[12, chunk(j)], w.at[13, chunk(j)], rf_s.at[j], rf_r.at[j],
              device(h, jnp.where(c == 0, down, up), c, x, l))
        for s in range(2):
            slot = pl.ds((8 if s == 0 else 0) + 2 * (1 - c), 2)
            bytes_wait(w.at[slot, chunk(j)], fw_r.at[j, s])

    def stage_of(p):
        j = jnp.where(p < 8, 0, jnp.where(p < 17, 1, 2))
        return j, jnp.where(p > 32, p - 33, p - pick(j, (4, 8, 15)))

    def corner(p):
        late = p > 34
        return (jnp.where(p < 17, p - 12, jnp.where(late, 0, (p - 17) // 2)),
                jnp.where(p < 17, 0, jnp.where(late, p - 34, 1 + (p - 19) % 2)))

    def in_stage(p):
        return ((p >= 4) & (p < 12)) | (p == 17) | (p == 18) | (p == 33) | (p == 34)

    def in_corner(p):
        return ((p >= 12) & (p < 17)) | ((p >= 19) & (p < 27)) | (p > 34)

    def cross_of(p):
        j, q = stage_of(p)
        v, u = corner(p)
        m = p - 27
        st, co = in_stage(p), in_corner(p)
        t = jnp.where(st, 0, jnp.where(co, (v + 1) // 2, 3))
        k = jnp.where(st, q - 2, jnp.where(co, (v + 1) % 2, m // 3))
        return t, k, jnp.where(st, j, jnp.where(co, u, m % 3))

    def is_cross(p):
        return (in_stage(p) & (stage_of(p)[1] >= 2)) | (in_corner(p) & (corner(p)[0] > 0)) | (
            (p > 26) & (p < 33))

    def same_of(p):
        j, q = stage_of(p)
        return jnp.where(p < 4, p, jnp.where(in_stage(p), 4 + 2 * j + q, 10 + corner(p)[1]))

    def unit_of_same(s):
        j, q = (s - 4) // 2, (s - 4) % 2
        return jnp.where(s < 4, s, jnp.where(s < 10, pick(j, (4, 8, 33)) + q,
                                             pick(s - 10, (12, 35, 36))))

    def multiply(p):
        cross = is_cross(p)
        j, q = stage_of(p)
        v, u = corner(p)
        t, k, part = cross_of(p)
        st, co = in_stage(p), in_corner(p)
        left = jnp.where(p < 2, own, jnp.where(p < 4, 4, jnp.where(st, own, 2 * c)))
        right = jnp.where(p < 2, own, jnp.where(p < 4, 6, jnp.where(st, 8 + 2 * q, 8 + 2 * c2)))
        o = 2 * (pick(t, (2, 4, 0, 4 * c)) + k) + h
        r = jnp.where(t == 3, 13, 12)
        left = jnp.where(cross, jnp.where(h == 0, o, r), left)
        right = jnp.where(cross, jnp.where(h == 0, r, o), right)
        row_wise = (cross & (t == 0) & (h == 1)) | (co & (u == 2))
        row = jnp.where(co, 2, j)
        col_wise = jnp.logical_not(row_wise | co | (p < 2))
        col = jnp.where(p == 2, c, jnp.where(p == 3, 2, jnp.where(st, j, p - 27) % 3))

        def gram(rows, cols, c0, c1, halves):
            total = None
            for half in range(halves):
                part = lax.dot_general(w[left + half, rows, c0:c1], w[right + half, cols, c0:c1],
                                       NT, preferred_element_type=jnp.float32)
                total = part if total is None else total + part
            return total.astype(jnp.bfloat16)

        def store(b, pa, qg):
            for a in range(2):
                for bb in range(2):
                    sl = slice((2 * a + bb) * QR, (2 * a + bb + 1) * QR)
                    xp[p, a, bb, b] = pa[sl]
                    xq[p, bb, a, b] = qg[sl]

        for halves in (1, 2):
            mine = cross if halves == 1 else jnp.logical_not(cross)
            whole = slice(None)

            @pl.when(mine & col_wise)
            def _():
                pa = gram(whole, chunk(col), 0, AH, halves)
                qg = gram(whole, chunk(col), AH, WH, halves)
                for b in range(3):
                    sl = slice(b * CH, (b + 1) * CH)
                    store(b, pa[sl], qg[sl])

            @pl.when(mine & row_wise)
            def _():
                pa = gram(chunk(row), whole, 0, AH, halves)
                qg = gram(chunk(row), whole, AH, WH, halves)
                for b in range(3):
                    sl = slice(b * CH, (b + 1) * CH)
                    store(b, pa[:, sl], qg[:, sl])

            @pl.when(mine & jnp.logical_not(row_wise | col_wise))
            def _():
                for b in range(3):
                    ib = jnp.where(u == 0, (0, 1, 1)[b], (0, 0, 1)[b])
                    jb = jnp.where(u == 0, (1, 0, 1)[b], (0, 2, 2)[b])
                    ib = jnp.where(p == 0, b, jnp.where(p == 1, (1, 2, 2)[b], ib))
                    jb = jnp.where(p == 0, b, jnp.where(p == 1, (0, 0, 1)[b], jb))
                    store(b, gram(chunk(ib), chunk(jb), 0, AH, halves),
                          gram(chunk(ib), chunk(jb), AH, WH, halves))

        start(xp.at[p, 1 - qa], rp.at[p], x1_s.at[0], x1_r.at[p, 0], device(h, y, c, xa, l))
        start(xq.at[p, 1 - qb], rq.at[p], x1_s.at[1], x1_r.at[p, 1], device(h, y, c, xb, l))

    def f32(v):
        return v.astype(jnp.float32)

    def exchange(p):
        bytes_wait(rp.at[p], x1_r.at[p, 0])
        sp2[p] = (f32(xp[p, qa, 1 - qb]) + f32(rp[p, 1 - qb])).astype(jnp.bfloat16)
        start(sp2.at[p], rp2.at[p], x2_s.at[0], x2_r.at[p, 0], device(h, y, c, xb, l))
        bytes_wait(rq.at[p], x1_r.at[p, 1])
        sq2[p] = (f32(xq[p, qb, 1 - qa]) + f32(rq[p, 1 - qa])).astype(jnp.bfloat16)
        start(sq2.at[p], rq2.at[p], x2_s.at[1], x2_r.at[p, 1], device(h, y, c, xa, l))

    def finish(p):
        bytes_wait(rp2.at[p], x2_r.at[p, 0])
        zs[p, :, :, 0:CH] = (f32(xp[p, qa, qb]) + f32(rp[p, qb]) + f32(rp2[p])).astype(jnp.bfloat16)
        bytes_wait(rq2.at[p], x2_r.at[p, 1])
        zs[p, :, :, CH:2 * CH] = (f32(xq[p, qb, qa]) + f32(rq[p, qa]) + f32(rq2[p])).astype(jnp.bfloat16)
        cross = is_cross(p)
        s = same_of(p)
        t, k, part = cross_of(p)
        mine = k == kept

        @pl.when(jnp.logical_not(cross) & (s % 4 != l))
        def _():
            o = s % 4
            start(zs.at[p], zr.at[s, (l - o + 3) % 4], z_s.at[p], z_r.at[s],
                  device(h, y, c, x, o))

        @pl.when(cross & mine & (t == l))
        def _():
            zc[zz, part] = zs[p]

        @pl.when(cross & jnp.logical_not(mine & (t == l)))
        def _():
            y2, t2 = other_side(t, k)
            dev = device(jnp.where(mine, h, 1 - h), jnp.where(mine, y, y2),
                         jnp.where(mine, c, k), x, jnp.where(mine, t, t2))
            start(zs.at[p], zc.at[zz, part], z_s.at[p], c_r, dev)

    row_id = lax.broadcasted_iota(jnp.int32, (SEQS, 128), 0)
    col_id = lax.broadcasted_iota(jnp.int32, (SEQS, 128), 1)

    def put(value, b, s):
        hit = ((row_id == b) & (col_id == s)) | ((row_id == s) & (col_id == b))
        return jnp.where(hit, value, 0.0)

    def seq(hh, yy, cc):
        return (hh * 4 + yy) * 2 + cc

    def keep_same(s):
        p = unit_of_same(s)

        @pl.when(s % 4 == l)
        def _():
            bytes_wait(zr.at[s], z_r.at[s])
            total = f32(zs[p])
            for d in range(3):
                total = total + f32(zr[s, d])
            value = jnp.sum(total[:, :, 0:CH] * total[:, :, CH:2 * CH])
            value = value * jnp.where(s == 1, 2.0, jnp.where(s == 3, 0.5, 1.0))
            b = jnp.where(s < 2, e, jnp.where(s < 4, seq(h, y, 0), jnp.where(
                s < 10, e, seq(h, down, c))))
            b2 = jnp.where(s < 2, e, jnp.where(s < 4, seq(h, y, 1), jnp.where(
                s < 10, seq(h, up, s % 2), seq(h, up, c2))))
            tb[0, in_plane] = tb[0, in_plane] + put(value, b, b2)

    tb[0, in_plane] = jnp.zeros((SEQS, 128), jnp.float32)

    @pl.loop(0, UNITS)
    def _(p):
        @pl.when(p == 2)
        def _():
            bytes_wait(w.at[pl.ds(own, 2)], sib_r)

        @pl.when(p == 4)
        def _():
            @pl.loop(0, 4)
            def _(i):
                exchange(p - 4 + i)

            @pl.loop(0, 4)
            def _(i):
                finish(p - 4 + i)

        @pl.when((p == 4) | (p == 8) | (p == 17))
        def _():
            arrive(stage_of(p)[0])

        @pl.when(p == 27)
        def _():
            for j in range(3):
                bytes_wait(w.at[13, chunk(j)], rf_r.at[j])

        multiply(p)

        @pl.when(p >= 4 + LAG)
        def _():
            exchange(p - LAG)

        @pl.when(p >= 4 + 2 * LAG)
        def _():
            finish(p - 2 * LAG)

        @pl.when(p == UNITS - 3)
        def _():
            @pl.loop(0, 8)
            def _(s):
                keep_same(s)

    @pl.loop(UNITS, UNITS + 2 * LAG)
    def _(p):
        @pl.when(p < UNITS + LAG)
        def _():
            exchange(p - LAG)

        finish(p - 2 * LAG)

    bytes_wait(zc.at[pl.ds(0, 7)], c_r)
    o_y = jnp.where(l == 0, y, jnp.where(l == 1, up, jnp.where(l == 2, down, (y + 4 - sgn) % 4)))
    r_y = jnp.where(l == 3, (y + 4 + sgn) % 4, y)

    def cross_block(i, acc):
        a, b = i // 3, i % 3
        a2, b2 = jnp.where(l == 0, b, a), jnp.where(l == 0, a, b)
        total = jnp.zeros((QR, 2 * CH), jnp.float32)
        for src in range(4):
            total = total + f32(zc[src, a2, b2])
        for src in range(4, 8):
            total = total + f32(zc[src, a, b])
        return acc + total[:, 0:CH] * total[:, CH:2 * CH]

    acc = lax.fori_loop(0, 9, cross_block, jnp.zeros((QR, CH), jnp.float32))
    tb[0, in_plane] = tb[0, in_plane] + put(
        jnp.sum(acc), seq(h, o_y, kept), seq(1 - h, r_y, c))

    @pl.loop(8, SAMES)
    def _(s):
        keep_same(s)

    def drain():
        bytes_wait(w.at[pl.ds(0, 2)], sib_s)
        for j in range(3):
            bytes_wait(w.at[0, chunk(j)], far_s.at[j])
            bytes_wait(w.at[0, chunk(j)], rf_s.at[j])
            for s in range(2):
                bytes_wait(w.at[pl.ds(0, 2), chunk(j)], y_s.at[j, s])
                bytes_wait(w.at[pl.ds(0, 2), chunk(j)], fw_s.at[j, s])
        bytes_wait(rp, x1_s.at[0])
        bytes_wait(rq, x1_s.at[1])
        bytes_wait(rp2, x2_s.at[0])
        bytes_wait(rq2, x2_s.at[1])

        @pl.loop(0, UNITS)
        def _(p):
            t, k, _ = cross_of(p)
            here = jnp.where(is_cross(p), (k == kept) & (t == l), same_of(p) % 4 == l)

            @pl.when(jnp.logical_not(here))
            def _():
                bytes_wait(zs.at[p], z_s.at[p])

    def add_up(s, me, dev_of):
        for d in range(1, 16):
            start(tb.at[s, me], tb.at[s, me], t_s.at[s], t_r.at[s], dev_of((me + d) % 16))
        if s == 0:
            drain()
        bytes_wait(tb.at[s, pl.ds(0, 15)], t_r.at[s])
        total = tb[s, 0]
        for d in range(1, 16):
            total = total + tb[s, d]
        return total

    tb[1, in_column] = add_up(0, in_plane, plane)
    total = add_up(1, in_column, column)
    line = jnp.sum(jnp.where(row_id == e, total, 0.0), axis=0, keepdims=True)
    out_ref[...] = line[:, 0:SEQS] / float(LEN * FF * D)

    for s in range(2):
        bytes_wait(tb.at[s, pl.ds(0, 15)], t_s.at[s])


def per_device(activations, out_grads, lengths):
    bf, dma = jnp.bfloat16, pltpu.SemaphoreType.DMA
    return pl.pallas_call(
        body,
        out_shape=jax.ShapeDtypeStruct((1, SEQS), jnp.float32),
        in_specs=[pl.BlockSpec(memory_space=pl.ANY), pl.BlockSpec(memory_space=pl.ANY),
                  pl.BlockSpec(memory_space=pltpu.SMEM)],
        out_specs=pl.BlockSpec(memory_space=pltpu.VMEM),
        scratch_shapes=[
            pltpu.VMEM((14, LEN, WH), bf),
            pltpu.VMEM((LEN, 2 * GH), bf),
            pltpu.VMEM((UNITS, 2, 2, 3, QR, CH), bf),
            pltpu.VMEM((UNITS, 2, 2, 3, QR, CH), bf),
            pltpu.VMEM((UNITS, 2, 3, QR, CH), bf),
            pltpu.VMEM((UNITS, 2, 3, QR, CH), bf),
            pltpu.VMEM((UNITS, 3, QR, CH), bf),
            pltpu.VMEM((UNITS, 3, QR, CH), bf),
            pltpu.VMEM((UNITS, 3, QR, CH), bf),
            pltpu.VMEM((UNITS, 3, QR, CH), bf),
            pltpu.VMEM((UNITS, 3, QR, 2 * CH), bf),
            pltpu.VMEM((SAMES, 3, 3, QR, 2 * CH), bf),
            pltpu.VMEM((8, 3, 3, QR, 2 * CH), bf),
            pltpu.VMEM((2, 16, SEQS, 128), jnp.float32),
            dma((3,)), dma, dma, dma((3,)), dma((3,)),
            dma((3, 2)), dma((3, 2)), dma((3, 2)), dma((3, 2)), dma((3,)), dma((3,)),
            dma((2,)), dma((UNITS, 2)), dma((2,)), dma((UNITS, 2)), dma((UNITS,)), dma((SAMES,)), dma,
            dma((2,)), dma((2,)),
        ],
        compiler_params=pltpu.CompilerParams(
            collective_id=0, has_side_effects=True, vmem_limit_bytes=56 << 20),
        name="ghost_kernel",
    )(activations, out_grads, lengths)


def solution(mesh):
    placed = (P("ex", "feat"), P("ex", "feat"), P("ex"))
    return jax.shard_map(
        per_device, mesh=mesh, in_specs=placed, out_specs=P("ex", None), check_vma=False
    )
```

```python
import jax
import jax.numpy as jnp
from jax import lax
from jax.experimental import pallas as pl
from jax.experimental.pallas import tpu as pltpu
from jax.sharding import PartitionSpec as P

FF = 28672
D = 8192
LEN = 384
SEQS = 16

MESH = pl.DeviceIdType.MESH
AH = FF // 32
GH = D // 32
WH = AH + GH
CH = 128
QR = CH // 4
UNITS = 37
SAMES = 13
LAG = 3
NT = (((1,), (1,)), ((), ()))


def device(h, y, c, x, l):
    return {"ex": (h * 4 + y) * 2 + c, "feat": x * 4 + l}


def bytes_wait(ref, sem):
    pltpu.make_async_copy(ref, ref, sem).wait()


def pick(index, values):
    out = values[-1]
    for i in range(len(values) - 2, -1, -1):
        out = jnp.where(index == i, values[i], out)
    return out


def body(act_ref, grad_ref, len_ref, out_ref, w, graw, xp, xq, rp, rq, sp2, sq2, rp2, rq2,
         zs, zr, zc, tb, in_sem, sib_s, sib_r, far_s, far_r, y_s, y_r, fw_s, fw_r, rf_s, rf_r,
         x1_s, x1_r, x2_s, x2_r, z_s, z_r, c_r, t_s, t_r):
    e = lax.axis_index("ex")
    f = lax.axis_index("feat")
    h, y, c = e // 8, (e // 2) % 4, e % 2
    x, l = f // 4, f % 4
    zz = h * 4 + l
    own = 4 + 2 * c
    up, down = (y + 1) % 4, (y + 3) % 4
    sgn = 1 - 2 * c
    qa, qb = ((x + 1) // 2) % 2, x // 2
    xa, xb = x + 1 - 2 * (x % 2), 3 - x
    c2 = jnp.where(y < 2, c, 1 - c)

    loads = []
    for half in range(2):
        loads.append(pltpu.make_async_copy(
            act_ref.at[:, pl.ds(half * AH, AH)], w.at[own + half, :, pl.ds(0, AH)],
            in_sem.at[half]))
    loads.append(pltpu.make_async_copy(grad_ref, graw, in_sem.at[2]))
    for ld in loads:
        ld.start()

    def other_side(t, k):
        o_shift = jnp.where(t == 0, 0, jnp.where(t == 1, 1, jnp.where(t == 2, 3, 4 - sgn)))
        y2 = jnp.where(t == 3, y + o_shift + 4 - (1 - 2 * k), y + o_shift) % 4
        t2 = jnp.where(t == 1, 2, jnp.where(t == 2, 1, t))
        return y2, t2

    kept = (c + h) % 2

    bar = pltpu.get_barrier_semaphore()

    def greet(dev):
        pl.semaphore_signal(bar, inc=1, device_id=dev, device_id_type=MESH)

    def plane(i):
        return device(h, i % 4, c, i // 4, l)

    def column(i):
        return device(i // 8, y, i % 2, x, (i // 2) % 4)

    in_plane, in_column = x * 4 + y, zz * 2 + c
    for d in range(1, 16):
        greet(plane((in_plane + d) % 16))
        greet(column((in_column + d) % 16))
    ysrc, _ = other_side(l, kept)
    for l2 in range(4):
        greet(device(1 - h, ysrc, kept, x, l2))

    for ld in loads:
        ld.wait()
    rows = lax.broadcasted_iota(jnp.int32, (LEN, GH), 0)
    valid = rows < len_ref[0]
    for half in range(2):
        g = graw[:, half * GH:(half + 1) * GH].astype(jnp.float32)
        w[own + half, :, AH:WH] = jnp.where(valid, g, 0.0).astype(jnp.bfloat16)
    pl.semaphore_wait(bar, 34)

    def start(src, dst, send, recv, dev):
        pltpu.make_async_remote_copy(src_ref=src, dst_ref=dst, send_sem=send, recv_sem=recv,
                                     device_id=dev, device_id_type=MESH).start()

    def chunk(j):
        return pl.ds(pl.multiple_of(j * CH, CH), CH)

    sibling = device(h, y, 1 - c, x, l)

    def send_far(j):
        start(w.at[own + 1 - h, chunk(j)], w.at[12, chunk(j)], far_s.at[j], far_r.at[j],
              device(1 - h, y, c, x, l))

    def send_near(j):
        start(w.at[pl.ds(own, 2), chunk(j)], w.at[pl.ds(8 + 2 * c, 2), chunk(j)],
              y_s.at[j, 0], y_r.at[j, 0], device(h, down, c, x, l))
        start(w.at[pl.ds(own, 2), chunk(j)], w.at[pl.ds(2 * c, 2), chunk(j)],
              y_s.at[j, 1], y_r.at[j, 1], device(h, up, c, x, l))

    for j in range(2):
        send_far(j)
        send_near(j)
    start(w.at[pl.ds(own, 2)], w.at[pl.ds(own, 2)], sib_s, sib_r, sibling)

    def arrive(j):
        for s in range(2):
            bytes_wait(w.at[pl.ds((8 if s == 0 else 0) + 2 * c, 2), chunk(j)], y_r.at[j, s])

        @pl.when(j < 1)
        def _():
            send_near(j + 2)

        for s in range(2):
            slot = pl.ds((8 if s == 0 else 0) + 2 * c, 2)
            start(w.at[slot, chunk(j)], w.at[slot, chunk(j)], fw_s.at[j, s], fw_r.at[j, s], sibling)
        bytes_wait(w.at[12, chunk(j)], far_r.at[j])

        @pl.when(j < 1)
        def _():
            send_far(j + 2)

        start(w.at[12, chunk(j)], w.at[13, chunk(j)], rf_s.at[j], rf_r.at[j],
              device(h, jnp.where(c == 0, down, up), c, x, l))

    def arrive_passed(j):
        for s in range(2):
            slot = pl.ds((8 if s == 0 else 0) + 2 * (1 - c), 2)
            bytes_wait(w.at[slot, chunk(j)], fw_r.at[j, s])

    def stage_of(p):
        j = jnp.where(p < 8, 0, jnp.where(p < 17, 1, 2))
        return j, jnp.where(p > 32, p - 33, jnp.where(p > 16, p - 15, (p + 2) % 4))

    def corner(p):
        late = p > 34
        return (jnp.where(p < 17, p - 12, jnp.where(late, 0, (p - 17) // 2)),
                jnp.where(p < 17, 0, jnp.where(late, p - 34, 1 + (p - 19) % 2)))

    def in_stage(p):
        return ((p >= 4) & (p < 12)) | (p == 17) | (p == 18) | (p == 33) | (p == 34)

    def in_corner(p):
        return ((p >= 12) & (p < 17)) | ((p >= 19) & (p < 27)) | (p > 34)

    def cross_of(p):
        j, q = stage_of(p)
        v, u = corner(p)
        m = p - 27
        st, co = in_stage(p), in_corner(p)
        t = jnp.where(st, 0, jnp.where(co, (v + 1) // 2, 3))
        k = jnp.where(st, q - 2, jnp.where(co, (v + 1) % 2, m // 3))
        return t, k, jnp.where(st, j, jnp.where(co, u, m % 3))

    def is_cross(p):
        return (in_stage(p) & (stage_of(p)[1] >= 2)) | (in_corner(p) & (corner(p)[0] > 0)) | (
            (p > 26) & (p < 33))

    def same_of(p):
        j, q = stage_of(p)
        return jnp.where(p < 4, p, jnp.where(in_stage(p), 4 + 2 * j + q, 10 + corner(p)[1]))

    def unit_of_same(s):
        j, q = (s - 4) // 2, (s - 4) % 2
        return jnp.where(s < 4, s, jnp.where(s < 10, pick(j, (6, 10, 33)) + q,
                                             pick(s - 10, (12, 35, 36))))

    def multiply(p):
        cross = is_cross(p)
        j, q = stage_of(p)
        v, u = corner(p)
        t, k, part = cross_of(p)
        st, co = in_stage(p), in_corner(p)
        left = jnp.where(p < 2, own, jnp.where(p < 4, 4, jnp.where(st, own, 2 * c)))
        right = jnp.where(p < 2, own, jnp.where(p < 4, 6, jnp.where(st, 8 + 2 * q, 8 + 2 * c2)))
        o = 2 * (pick(t, (2, 4, 0, 4 * c)) + k) + h
        r = jnp.where(t == 3, 13, 12)
        left = jnp.where(cross, jnp.where(h == 0, o, r), left)
        right = jnp.where(cross, jnp.where(h == 0, r, o), right)
        row_wise = (cross & (t == 0) & (h == 1)) | (co & (u == 2))
        row = jnp.where(co, 2, j)
        col_wise = jnp.logical_not(row_wise | co | (p < 2))
        col = jnp.where(p == 2, c, jnp.where(p == 3, 2, jnp.where(st, j, p - 27) % 3))

        def gram(rows, cols, c0, c1, halves):
            total = None
            for half in range(halves):
                part = lax.dot_general(w[left + half, rows, c0:c1], w[right + half, cols, c0:c1],
                                       NT, preferred_element_type=jnp.float32)
                total = part if total is None else total + part
            return total.astype(jnp.bfloat16)

        def store(b, pa, qg):
            for a in range(2):
                for bb in range(2):
                    sl = slice((2 * a + bb) * QR, (2 * a + bb + 1) * QR)
                    xp[p, a, bb, b] = pa[sl]
                    xq[p, bb, a, b] = qg[sl]

        for halves in (1, 2):
            mine = cross if halves == 1 else jnp.logical_not(cross)
            whole = slice(None)

            @pl.when(mine & col_wise)
            def _():
                pa = gram(whole, chunk(col), 0, AH, halves)
                qg = gram(whole, chunk(col), AH, WH, halves)
                for b in range(3):
                    sl = slice(b * CH, (b + 1) * CH)
                    store(b, pa[sl], qg[sl])

            @pl.when(mine & row_wise)
            def _():
                pa = gram(chunk(row), whole, 0, AH, halves)
                qg = gram(chunk(row), whole, AH, WH, halves)
                for b in range(3):
                    sl = slice(b * CH, (b + 1) * CH)
                    store(b, pa[:, sl], qg[:, sl])

            @pl.when(mine & jnp.logical_not(row_wise | col_wise))
            def _():
                for b in range(3):
                    ib = jnp.where(u == 0, (0, 1, 1)[b], (0, 0, 1)[b])
                    jb = jnp.where(u == 0, (1, 0, 1)[b], (0, 2, 2)[b])
                    ib = jnp.where(p == 0, b, jnp.where(p == 1, (1, 2, 2)[b], ib))
                    jb = jnp.where(p == 0, b, jnp.where(p == 1, (0, 0, 1)[b], jb))
                    store(b, gram(chunk(ib), chunk(jb), 0, AH, halves),
                          gram(chunk(ib), chunk(jb), AH, WH, halves))

        start(xp.at[p, 1 - qa], rp.at[p], x1_s.at[0], x1_r.at[p, 0], device(h, y, c, xa, l))
        start(xq.at[p, 1 - qb], rq.at[p], x1_s.at[1], x1_r.at[p, 1], device(h, y, c, xb, l))

    def f32(v):
        return v.astype(jnp.float32)

    def exchange(p):
        bytes_wait(rp.at[p], x1_r.at[p, 0])
        sp2[p] = (f32(xp[p, qa, 1 - qb]) + f32(rp[p, 1 - qb])).astype(jnp.bfloat16)
        start(sp2.at[p], rp2.at[p], x2_s.at[0], x2_r.at[p, 0], device(h, y, c, xb, l))
        bytes_wait(rq.at[p], x1_r.at[p, 1])
        sq2[p] = (f32(xq[p, qb, 1 - qa]) + f32(rq[p, 1 - qa])).astype(jnp.bfloat16)
        start(sq2.at[p], rq2.at[p], x2_s.at[1], x2_r.at[p, 1], device(h, y, c, xa, l))

    def finish(p):
        bytes_wait(rp2.at[p], x2_r.at[p, 0])
        zs[p, :, :, 0:CH] = (f32(xp[p, qa, qb]) + f32(rp[p, qb]) + f32(rp2[p])).astype(jnp.bfloat16)
        bytes_wait(rq2.at[p], x2_r.at[p, 1])
        zs[p, :, :, CH:2 * CH] = (f32(xq[p, qb, qa]) + f32(rq[p, qa]) + f32(rq2[p])).astype(jnp.bfloat16)
        cross = is_cross(p)
        s = same_of(p)
        t, k, part = cross_of(p)
        mine = k == kept

        @pl.when(jnp.logical_not(cross) & (s % 4 != l))
        def _():
            o = s % 4
            start(zs.at[p], zr.at[s, (l - o + 3) % 4], z_s.at[p], z_r.at[s],
                  device(h, y, c, x, o))

        @pl.when(cross & mine & (t == l))
        def _():
            zc[zz, part] = zs[p]

        @pl.when(cross & jnp.logical_not(mine & (t == l)))
        def _():
            y2, t2 = other_side(t, k)
            dev = device(jnp.where(mine, h, 1 - h), jnp.where(mine, y, y2),
                         jnp.where(mine, c, k), x, jnp.where(mine, t, t2))
            start(zs.at[p], zc.at[zz, part], z_s.at[p], c_r, dev)

    row_id = lax.broadcasted_iota(jnp.int32, (SEQS, 128), 0)
    col_id = lax.broadcasted_iota(jnp.int32, (SEQS, 128), 1)

    def put(value, b, s):
        hit = ((row_id == b) & (col_id == s)) | ((row_id == s) & (col_id == b))
        return jnp.where(hit, value, 0.0)

    def seq(hh, yy, cc):
        return (hh * 4 + yy) * 2 + cc

    def keep_same(s):
        p = unit_of_same(s)

        @pl.when(s % 4 == l)
        def _():
            bytes_wait(zr.at[s], z_r.at[s])
            total = f32(zs[p])
            for d in range(3):
                total = total + f32(zr[s, d])
            value = jnp.sum(total[:, :, 0:CH] * total[:, :, CH:2 * CH])
            value = value * jnp.where(s == 1, 2.0, jnp.where(s == 3, 0.5, 1.0))
            b = jnp.where(s < 2, e, jnp.where(s < 4, seq(h, y, 0), jnp.where(
                s < 10, e, seq(h, down, c))))
            b2 = jnp.where(s < 2, e, jnp.where(s < 4, seq(h, y, 1), jnp.where(
                s < 10, seq(h, up, s % 2), seq(h, up, c2))))
            tb[0, in_plane] = tb[0, in_plane] + put(value, b, b2)

    tb[0, in_plane] = jnp.zeros((SEQS, 128), jnp.float32)

    @pl.loop(0, UNITS)
    def _(p):
        @pl.when(p == 2)
        def _():
            bytes_wait(w.at[pl.ds(own, 2)], sib_r)

        @pl.when(p == 4)
        def _():
            @pl.loop(0, 4)
            def _(i):
                exchange(p - 4 + i)

            @pl.loop(0, 4)
            def _(i):
                finish(p - 4 + i)

        @pl.when((p == 4) | (p == 8) | (p == 17))
        def _():
            arrive(stage_of(p)[0])

        @pl.when((p == 6) | (p == 10) | (p == 19))
        def _():
            arrive_passed(jnp.where(p == 6, 0, jnp.where(p == 10, 1, 2)))

        @pl.when(p == 27)
        def _():
            for j in range(3):
                bytes_wait(w.at[13, chunk(j)], rf_r.at[j])

        multiply(p)

        @pl.when(p >= 4 + LAG)
        def _():
            exchange(p - LAG)

        @pl.when(p >= 4 + 2 * LAG)
        def _():
            finish(p - 2 * LAG)

        @pl.when(p == UNITS - 3)
        def _():
            @pl.loop(0, 8)
            def _(s):
                keep_same(s)

    @pl.loop(UNITS, UNITS + 2 * LAG)
    def _(p):
        @pl.when(p < UNITS + LAG)
        def _():
            exchange(p - LAG)

        finish(p - 2 * LAG)

    bytes_wait(zc.at[pl.ds(0, 7)], c_r)
    o_y = jnp.where(l == 0, y, jnp.where(l == 1, up, jnp.where(l == 2, down, (y + 4 - sgn) % 4)))
    r_y = jnp.where(l == 3, (y + 4 + sgn) % 4, y)

    def cross_block(i, acc):
        a, b = i // 3, i % 3
        a2, b2 = jnp.where(l == 0, b, a), jnp.where(l == 0, a, b)
        total = jnp.zeros((QR, 2 * CH), jnp.float32)
        for src in range(4):
            total = total + f32(zc[src, a2, b2])
        for src in range(4, 8):
            total = total + f32(zc[src, a, b])
        return acc + total[:, 0:CH] * total[:, CH:2 * CH]

    acc = lax.fori_loop(0, 9, cross_block, jnp.zeros((QR, CH), jnp.float32))
    tb[0, in_plane] = tb[0, in_plane] + put(
        jnp.sum(acc), seq(h, o_y, kept), seq(1 - h, r_y, c))

    @pl.loop(8, SAMES)
    def _(s):
        keep_same(s)

    def drain():
        bytes_wait(w.at[pl.ds(0, 2)], sib_s)
        for j in range(3):
            bytes_wait(w.at[0, chunk(j)], far_s.at[j])
            bytes_wait(w.at[0, chunk(j)], rf_s.at[j])
            for s in range(2):
                bytes_wait(w.at[pl.ds(0, 2), chunk(j)], y_s.at[j, s])
                bytes_wait(w.at[pl.ds(0, 2), chunk(j)], fw_s.at[j, s])
        bytes_wait(rp, x1_s.at[0])
        bytes_wait(rq, x1_s.at[1])
        bytes_wait(rp2, x2_s.at[0])
        bytes_wait(rq2, x2_s.at[1])

        @pl.loop(0, UNITS)
        def _(p):
            t, k, _ = cross_of(p)
            here = jnp.where(is_cross(p), (k == kept) & (t == l), same_of(p) % 4 == l)

            @pl.when(jnp.logical_not(here))
            def _():
                bytes_wait(zs.at[p], z_s.at[p])

    def add_up(s, me, dev_of):
        for d in range(1, 16):
            start(tb.at[s, me], tb.at[s, me], t_s.at[s], t_r.at[s], dev_of((me + d) % 16))
        if s == 0:
            drain()
        bytes_wait(tb.at[s, pl.ds(0, 15)], t_r.at[s])
        total = tb[s, 0]
        for d in range(1, 16):
            total = total + tb[s, d]
        return total

    tb[1, in_column] = add_up(0, in_plane, plane)
    total = add_up(1, in_column, column)
    line = jnp.sum(jnp.where(row_id == e, total, 0.0), axis=0, keepdims=True)
    out_ref[...] = line[:, 0:SEQS] / float(LEN * FF * D)

    for s in range(2):
        bytes_wait(tb.at[s, pl.ds(0, 15)], t_s.at[s])


def per_device(activations, out_grads, lengths):
    bf, dma = jnp.bfloat16, pltpu.SemaphoreType.DMA
    return pl.pallas_call(
        body,
        out_shape=jax.ShapeDtypeStruct((1, SEQS), jnp.float32),
        in_specs=[pl.BlockSpec(memory_space=pl.ANY), pl.BlockSpec(memory_space=pl.ANY),
                  pl.BlockSpec(memory_space=pltpu.SMEM)],
        out_specs=pl.BlockSpec(memory_space=pltpu.VMEM),
        scratch_shapes=[
            pltpu.VMEM((14, LEN, WH), bf),
            pltpu.VMEM((LEN, 2 * GH), bf),
            pltpu.VMEM((UNITS, 2, 2, 3, QR, CH), bf),
            pltpu.VMEM((UNITS, 2, 2, 3, QR, CH), bf),
            pltpu.VMEM((UNITS, 2, 3, QR, CH), bf),
            pltpu.VMEM((UNITS, 2, 3, QR, CH), bf),
            pltpu.VMEM((UNITS, 3, QR, CH), bf),
            pltpu.VMEM((UNITS, 3, QR, CH), bf),
            pltpu.VMEM((UNITS, 3, QR, CH), bf),
            pltpu.VMEM((UNITS, 3, QR, CH), bf),
            pltpu.VMEM((UNITS, 3, QR, 2 * CH), bf),
            pltpu.VMEM((SAMES, 3, 3, QR, 2 * CH), bf),
            pltpu.VMEM((8, 3, 3, QR, 2 * CH), bf),
            pltpu.VMEM((2, 16, SEQS, 128), jnp.float32),
            dma((3,)), dma, dma, dma((3,)), dma((3,)),
            dma((3, 2)), dma((3, 2)), dma((3, 2)), dma((3, 2)), dma((3,)), dma((3,)),
            dma((2,)), dma((UNITS, 2)), dma((2,)), dma((UNITS, 2)), dma((UNITS,)), dma((SAMES,)), dma,
            dma((2,)), dma((2,)),
        ],
        compiler_params=pltpu.CompilerParams(
            collective_id=0, has_side_effects=True, vmem_limit_bytes=56 << 20),
        name="ghost_kernel",
    )(activations, out_grads, lengths)


def solution(mesh):
    placed = (P("ex", "feat"), P("ex", "feat"), P("ex"))
    return jax.shard_map(
        per_device, mesh=mesh, in_specs=placed, out_specs=P("ex", None), check_vma=False
    )
```
